256 devices in a mesh: path: 32 (over y, x, core), shard: 8 (over z).
Axes of the slice: x: 4, y: 4, z: 8, core: 2. Of those that a mesh axis runs over, the one named last changes fastest.
Arguments:
- trained: bfloat16 [32, 4096, 2048], P('path', 'shard'), may hold values from -0.09375 to 0.09375
- outer_params: float32 [8, 8, 512, 2048], P(None, 'shard', 'path'), may hold values from -0.09375 to 0.09375
- momentum: float32 [8, 8, 512, 2048], P(None, 'shard', 'path'), may hold values from -0.12 to 0.12
- path_module: int32 [32, 1], replicated, may hold values from 0 to 7
- module_slot: int32 [8], replicated, may hold values from 0 to 7, each once
- hidden: bfloat16 [32, 2048, 4096], P('path', None, 'shard'), may hold values from -6 to 6
- residual: bfloat16 [32, 2048, 2048], P('path', 'shard'), may hold values from -6 to 6
Outputs:
- new_params: float32 [8, 8, 512, 2048], P(None, 'shard', 'path')
- new_momentum: float32 [8, 8, 512, 2048], P(None, 'shard', 'path')
- new_slabs: bfloat16 [32, 4096, 2048], P('path', 'shard')
- mixed: bfloat16 [32, 2048, 2048], P('path', 'shard')
The draws below stay inside these ranges and needn't reach their ends.
Inputs may be any that keep to these rules, and one draw needn't show every extreme that they name: `path_module`: every module is used by at least one path. `module_slot`: each slot holds exactly one module.
All inputs are finite; a program needn't handle non-finite values.
Results may differ from the reference program's by a relative error of at most 0.015.
Values may be sent and summed in bfloat16 or wider, within the bound.
No kernel may reach another device: no remote copies, remote signals or barrier semaphores. Data moves between devices by JAX's collectives and lax.ppermute only.
A program may use at most 128 MiB of HBM per device.

```python
import jax
import jax.numpy as jnp
from jax import lax

D = 2048
FFW = 4096
MODS = 8
TOK = 2048
PATHS = 32
SLABS = 8
ROWS = 512


def shard_levels(rng, extent, pieces, smallest, top_value):
    loudness, own = 1.0, jax.random.fold_in(rng, 6)
    for dim, shards_of in pieces:
        heights = jnp.exp(jax.random.uniform(jax.random.fold_in(own, dim), (shards_of,), jnp.float32, smallest / len(pieces), top_value / len(pieces)))
        loudness = loudness * jnp.repeat(heights, extent[dim] // shards_of).reshape([-1 if axis == dim else 1 for axis in range(len(extent))])
    return loudness


def picks_of(own_key, rows, count, top, lift):
    order = jax.random.permutation(jax.random.fold_in(own_key, 1), count)
    boost = order
    for power in range(3):
        boost = boost * boost // count
    boost = boost * lift // count
    tickets = jax.random.randint(jax.random.fold_in(own_key, 2), (rows, count), 0, 4096) + boost
    sure = jax.random.permutation(jax.random.fold_in(own_key, 3), rows)[jnp.arange(count) % rows]
    tickets = jnp.where(jnp.arange(rows)[:, None] == sure[None, :], 1 << 14, tickets)
    score = tickets * count + jnp.arange(count)
    return lax.top_k(score.astype(jnp.int32), top)[1].astype(jnp.int32)


def normal_values(stream_key, extent, scale, limit, shards=(), held_as=jnp.bfloat16):
    drawn = scale * jax.random.normal(stream_key, extent, jnp.float32)
    if shards:
        drawn = drawn * shard_levels(stream_key, extent, shards, -0.22, 0.18)
    return jnp.clip(drawn, -limit, limit).astype(held_as)


def setup_inputs(seed: int = 0) -> dict:
    arg_keys = jax.random.split(jax.random.key(seed), 8)
    trained = normal_values(arg_keys[0], (PATHS, FFW, D), FFW ** -0.5, 0.09375, ((0, 32), (1, 8)))
    outer_params = normal_values(arg_keys[1], (MODS, SLABS, ROWS, D), FFW ** -0.5, 0.09375, ((1, 8), (2, 32)), jnp.float32)
    momentum = normal_values(arg_keys[2], (MODS, SLABS, ROWS, D), 0.02, 0.12, ((1, 8), (2, 32)), jnp.float32)
    path_module = picks_of(arg_keys[3], PATHS, MODS, 1, 2048)
    module_slot = jax.random.permutation(arg_keys[4], MODS).astype(jnp.int32)
    hidden = normal_values(arg_keys[5], (PATHS, TOK, FFW), 1.0, 6.0, ((0, 32), (2, 8)))
    residual = normal_values(arg_keys[6], (PATHS, TOK, D), 1.0, 6.0, ((0, 32), (1, 8)))
    return dict(trained=trained, outer_params=outer_params, momentum=momentum, path_module=path_module, module_slot=module_slot, hidden=hidden, residual=residual)


def reference(trained, outer_params, momentum, path_module, module_slot, hidden, residual):
    slot_of_path = module_slot[path_module[:, 0]]
    choose = slot_of_path[None, :] == jnp.arange(MODS, dtype=jnp.int32)[:, None]
    counts = jnp.sum(choose.astype(jnp.float32), axis=1)
    flat = trained.reshape(PATHS, FFW * D)
    totals = jnp.dot(choose.astype(jnp.bfloat16), flat, preferred_element_type=jnp.float32)
    average = (totals / counts[:, None]).reshape(outer_params.shape)
    pseudo = outer_params - average
    new_momentum = 0.9 * momentum + pseudo
    new_params = outer_params - 0.7 * (pseudo + 0.9 * new_momentum)
    weights = new_params.astype(jnp.bfloat16).reshape(MODS, FFW, D)
    new_slabs = weights[slot_of_path]

    def one_path(items):
        rows_in, slab, resid = items
        total = jnp.zeros((TOK, D), jnp.float32)
        for block in range(SLABS):
            part = jnp.dot(rows_in[:, block * ROWS:(block + 1) * ROWS], slab[block * ROWS:(block + 1) * ROWS], preferred_element_type=jnp.float32)
            rounded = lax.optimization_barrier(part.astype(jnp.bfloat16))
            total = total + rounded.astype(jnp.float32)
        return (resid.astype(jnp.float32) + total).astype(jnp.bfloat16)

    mixed = lax.map(one_path, (hidden, new_slabs, residual))
    return new_params, new_momentum, new_slabs, mixed
```

```python
import jax
import jax.numpy as jnp
from jax import lax
from jax.experimental import pallas as pl
from jax.experimental.pallas import tpu as pltpu
from jax.sharding import PartitionSpec as P

STREAMS = (1024, 1024)
HEADS = True
WIDE = 256
LIMIT = 12


def after(value, *others):
    return lax.optimization_barrier((value, *others))[0]


def update_kernel(pick, back, count, received, outer, moment, params, moments, sent):
    totals = jnp.dot(pick[...], received[...], preferred_element_type=jnp.float32)
    pseudo = outer[...] - totals / count[...]
    momentum = 0.9 * moment[...] + pseudo
    new = outer[...] - 0.7 * (pseudo + 0.9 * momentum)
    params[...] = new
    moments[...] = momentum
    sent[...] = jnp.dot(
        back[...], new.astype(jnp.bfloat16), preferred_element_type=jnp.float32
    ).astype(jnp.bfloat16)


def update(pick, back, count, received, outer, moment):
    held, width = outer.shape
    rows = received.shape[0]
    wide = WIDE
    fixed = lambda i: (0, 0)
    here = lambda i: (0, i)
    return pl.pallas_call(
        update_kernel,
        grid=(width // wide,),
        in_specs=[
            pl.BlockSpec(pick.shape, fixed),
            pl.BlockSpec(back.shape, fixed),
            pl.BlockSpec(count.shape, fixed),
            pl.BlockSpec((rows, wide), here),
            pl.BlockSpec((held, wide), here),
            pl.BlockSpec((held, wide), here),
        ],
        out_specs=[
            pl.BlockSpec((held, wide), here),
            pl.BlockSpec((held, wide), here),
            pl.BlockSpec((rows, wide), here),
        ],
        out_shape=[
            pltpu.HBM((held, width), jnp.float32),
            pltpu.HBM((held, width), jnp.float32),
            pltpu.HBM((rows, width), jnp.bfloat16),
        ],
        compiler_params=pltpu.CompilerParams(vmem_limit_bytes=LIMIT * 1024 * 1024),
        cost_estimate=pl.CostEstimate(
            flops=4 * held * rows * width,
            bytes_accessed=(rows * 4 + held * 16) * width,
            transcendentals=0,
        ),
        name="update",
    )(pick, back, count, received, outer, moment)


def product_kernel(place, hidden, slab, *rest):
    outs, slabs, total = rest[-8:-2], rest[-2], rest[-1]
    total[...] = jnp.dot(hidden[...], slab[...], preferred_element_type=jnp.float32).astype(
        total.dtype
    )
    slabs[...] = slab[...]
    tokens = outs[0].shape[0]
    shards = hidden.shape[0] // tokens
    far = shards // 2
    for d, out in zip([d for d in range(shards) if d not in (far, far + 1)], outs):
        start = pl.multiple_of(place[d] * tokens, tokens)
        out[...] = total[pl.ds(start, tokens), :]


def products(place, hidden, slab, earlier, at, w, shards):
    rows, width = slab.shape
    tokens = hidden.shape[0] // shards
    wide = WIDE
    first = at // wide
    outs = pl.pallas_call(
        product_kernel,
        grid_spec=pltpu.PrefetchScalarGridSpec(
            num_scalar_prefetch=1,
            grid=(w // wide,),
            in_specs=[
                pl.BlockSpec(hidden.shape, lambda j, p: (0, 0)),
                pl.BlockSpec((rows, wide), lambda j, p: (0, first + j)),
            ]
            + [pl.BlockSpec(memory_space=pl.ANY)] * len(earlier),
            out_specs=[pl.BlockSpec((tokens, wide), lambda j, p: (0, j))] * (shards - 2)
            + [pl.BlockSpec((rows, wide), lambda j, p: (0, first + j))],
            scratch_shapes=[pltpu.VMEM((hidden.shape[0], wide), jnp.bfloat16)],
        ),
        out_shape=[jax.ShapeDtypeStruct((tokens, w), jnp.bfloat16)] * (shards - 2)
        + [pltpu.HBM((rows, width), jnp.bfloat16)],
        input_output_aliases={3: shards - 2} if earlier else {},
        compiler_params=pltpu.CompilerParams(vmem_limit_bytes=LIMIT * 1024 * 1024),
        cost_estimate=pl.CostEstimate(
            flops=2 * hidden.size * w,
            bytes_accessed=2 * (hidden.size + 2 * rows * w + shards * tokens * w),
            transcendentals=0,
        ),
        name="products",
    )(place, hidden, slab, *earlier)
    return list(outs[:-1]), outs[-1]


def body(trained, outer_params, momentum, path_module, module_slot, hidden, residual):
    paths = lax.axis_size("path")
    shards = lax.axis_size("shard")
    mods = outer_params.shape[0]
    piece = outer_params.shape[2]
    width = outer_params.shape[3]
    rows = paths * piece
    held = mods * piece
    labels = jnp.arange(mods, dtype=jnp.int32)
    slot_of_path = jnp.sum(
        jnp.where(path_module == labels[None, :], module_slot[None, :], 0), axis=1
    )
    choose = slot_of_path[None, :] == labels[:, None]
    counts = jnp.sum(choose.astype(jnp.float32), axis=1)
    count_of_row = jnp.repeat(counts, piece)[:, None]
    row_of_held = jnp.arange(held, dtype=jnp.int32)
    row_of_all = jnp.arange(rows, dtype=jnp.int32)
    slot_of_row = jnp.repeat(slot_of_path, piece) * piece + row_of_all % piece
    pick = (row_of_held[:, None] == slot_of_row[None, :]).astype(jnp.bfloat16)
    back = (slot_of_row[:, None] == row_of_held[None, :]).astype(jnp.bfloat16)

    def exchange(block):
        w = block.shape[1]
        return lax.all_to_all(
            block.reshape(paths, piece, w), "path", split_axis=0, concat_axis=0, tiled=True
        ).reshape(rows, w)

    outer = outer_params.reshape(held, width)
    moment = momentum.reshape(held, width)
    rows_in = hidden[0]
    z = lax.axis_index("shard")
    tokens = residual.shape[1]
    up = [(i, (i + 1) % shards) for i in range(shards)]
    down = [(i, (i - 1) % shards) for i in range(shards)]
    far = shards // 2
    ring_width = sum(STREAMS)

    received = exchange(trained[0])
    params, moments, sent = update(pick, back, count_of_row, received, outer, moment)
    slab = exchange(sent)

    def add(part, value):
        return (part.astype(jnp.float32) + value.astype(jnp.float32)).astype(jnp.bfloat16)

    class Ring:
        def __init__(self, lo, w, flip):
            self.lo, self.w = lo, w
            self.one, self.other = (down, up) if flip else (up, down)
            self.sign = -1 if flip else 1
            self.ahead, self.behind = self.head(far), self.head(far + 1)

        def head(self, offset):
            at = (z + self.sign * offset) % shards * tokens
            block = lax.dynamic_slice_in_dim(rows_in, at, tokens, 0)
            part = jnp.dot(
                block, slab[:, self.lo:self.lo + self.w], preferred_element_type=jnp.float32
            )
            return part.astype(jnp.bfloat16)

        def run(self, slab, earlier):
            place = ((z + self.sign * jnp.arange(shards, dtype=jnp.int32)) % shards).astype(jnp.int32)
            parts, whole = products(place, rows_in, slab, earlier, self.lo, self.w, shards)
            parts = parts[:far] + [None, None] + parts[far:]
            for k in range(far - 1, 0, -1):
                self.ahead = add(parts[k], lax.ppermute(self.ahead, "shard", self.one))
            for k in range(far - 2, 0, -1):
                self.behind = add(parts[shards - k], lax.ppermute(self.behind, "shard", self.other))
            ahead = lax.ppermute(self.ahead, "shard", self.one)
            behind = lax.ppermute(self.behind, "shard", self.other)
            own = parts[0].astype(jnp.float32)
            own = own + residual[0, :, self.lo:self.lo + self.w].astype(jnp.float32)
            self.total = (own + ahead.astype(jnp.float32) + behind.astype(jnp.float32)).astype(
                jnp.bfloat16
            )
            return [whole]

    rings, lo = [], 0
    for n, w in enumerate(STREAMS):
        rings.append(Ring(lo, w, n % 2 == 1))
        lo += w
    if HEADS:
        later = after(slab, *[r.ahead for r in rings], *[r.behind for r in rings])
    else:
        later = slab
    whole = []
    for r in rings:
        whole = r.run(later, whole)
    mixed = [r.total for r in rings]
    return (
        params.reshape(outer_params.shape),
        moments.reshape(outer_params.shape),
        whole[0][None],
        jnp.concatenate(mixed, axis=1)[None],
    )


def solution(mesh):
    placed = (
        P("path", "shard", None),
        P(None, "shard", "path", None),
        P(None, "shard", "path", None),
        P(),
        P(),
        P("path", None, "shard"),
        P("path", "shard", None),
    )
    return jax.shard_map(
        body,
        mesh=mesh,
        in_specs=placed,
        out_specs=(
            P(None, "shard", "path", None),
            P(None, "shard", "path", None),
            P("path", "shard", None),
            P("path", "shard", None),
        ),
        check_vma=False,
    )
```

```python
import jax
import jax.numpy as jnp
from jax import lax
from jax.experimental import pallas as pl
from jax.experimental.pallas import tpu as pltpu
from jax.sharding import PartitionSpec as P

STREAMS = (768, 768, 512)
WIDE = 256
LIMIT = 12
UPW = 512


def after(value, *others):
    return lax.optimization_barrier((value, *others))[0]


def update_kernel(pick, back, count, received, outer, moment, params, moments, sent):
    totals = jnp.dot(pick[...], received[...], preferred_element_type=jnp.float32)
    pseudo = outer[...] - totals / count[...]
    momentum = 0.9 * moment[...] + pseudo
    new = outer[...] - 0.7 * (pseudo + 0.9 * momentum)
    params[...] = new
    moments[...] = momentum
    sent[...] = jnp.dot(
        back[...], new.astype(jnp.bfloat16), preferred_element_type=jnp.float32
    ).astype(jnp.bfloat16)


def update(pick, back, count, received, outer, moment):
    held, width = outer.shape
    rows = received.shape[0]
    wide = UPW
    fixed = lambda i: (0, 0)
    here = lambda i: (0, i)
    return pl.pallas_call(
        update_kernel,
        grid=(width // wide,),
        in_specs=[
            pl.BlockSpec(pick.shape, fixed),
            pl.BlockSpec(back.shape, fixed),
            pl.BlockSpec(count.shape, fixed),
            pl.BlockSpec((rows, wide), here),
            pl.BlockSpec((held, wide), here),
            pl.BlockSpec((held, wide), here),
        ],
        out_specs=[
            pl.BlockSpec((held, wide), here),
            pl.BlockSpec((held, wide), here),
            pl.BlockSpec((rows, wide), here),
        ],
        out_shape=[
            pltpu.HBM((held, width), jnp.float32),
            pltpu.HBM((held, width), jnp.float32),
            pltpu.HBM((rows, width), jnp.bfloat16),
        ],
        compiler_params=pltpu.CompilerParams(vmem_limit_bytes=LIMIT * 1024 * 1024),
        cost_estimate=pl.CostEstimate(
            flops=4 * held * rows * width,
            bytes_accessed=(rows * 4 + held * 16) * width,
            transcendentals=0,
        ),
        name="update",
    )(pick, back, count, received, outer, moment)


def product_kernel(place, hidden, slab, *rest):
    outs, slabs, total = rest[-8:-2], rest[-2], rest[-1]
    total[...] = jnp.dot(hidden[...], slab[...], preferred_element_type=jnp.float32).astype(
        total.dtype
    )
    slabs[...] = slab[...]
    tokens = outs[0].shape[0]
    shards = hidden.shape[0] // tokens
    far = shards // 2
    for d, out in zip([d for d in range(shards) if d not in (far, far + 1)], outs):
        start = pl.multiple_of(place[d] * tokens, tokens)
        out[...] = total[pl.ds(start, tokens), :]


def products(place, hidden, slab, earlier, at, w, shards):
    rows, width = slab.shape
    tokens = hidden.shape[0] // shards
    wide = WIDE
    first = at // wide
    outs = pl.pallas_call(
        product_kernel,
        grid_spec=pltpu.PrefetchScalarGridSpec(
            num_scalar_prefetch=1,
            grid=(w // wide,),
            in_specs=[
                pl.BlockSpec(hidden.shape, lambda j, p: (0, 0)),
                pl.BlockSpec((rows, wide), lambda j, p: (0, first + j)),
            ]
            + [pl.BlockSpec(memory_space=pl.ANY)] * len(earlier),
            out_specs=[pl.BlockSpec((tokens, wide), lambda j, p: (0, j))] * (shards - 2)
            + [pl.BlockSpec((rows, wide), lambda j, p: (0, first + j))],
            scratch_shapes=[pltpu.VMEM((hidden.shape[0], wide), jnp.bfloat16)],
        ),
        out_shape=[jax.ShapeDtypeStruct((tokens, w), jnp.bfloat16)] * (shards - 2)
        + [pltpu.HBM((rows, width), jnp.bfloat16)],
        input_output_aliases={3: shards - 2} if earlier else {},
        compiler_params=pltpu.CompilerParams(vmem_limit_bytes=LIMIT * 1024 * 1024),
        cost_estimate=pl.CostEstimate(
            flops=2 * hidden.size * w,
            bytes_accessed=2 * (hidden.size + 2 * rows * w + shards * tokens * w),
            transcendentals=0,
        ),
        name="products",
    )(place, hidden, slab, *earlier)
    return list(outs[:-1]), outs[-1]


def body(trained, outer_params, momentum, path_module, module_slot, hidden, residual):
    paths = lax.axis_size("path")
    shards = lax.axis_size("shard")
    mods = outer_params.shape[0]
    piece = outer_params.shape[2]
    width = outer_params.shape[3]
    rows = paths * piece
    held = mods * piece
    labels = jnp.arange(mods, dtype=jnp.int32)
    slot_of_path = jnp.sum(
        jnp.where(path_module == labels[None, :], module_slot[None, :], 0), axis=1
    )
    choose = slot_of_path[None, :] == labels[:, None]
    counts = jnp.sum(choose.astype(jnp.float32), axis=1)
    count_of_row = jnp.repeat(counts, piece)[:, None]
    row_of_held = jnp.arange(held, dtype=jnp.int32)
    row_of_all = jnp.arange(rows, dtype=jnp.int32)
    slot_of_row = jnp.repeat(slot_of_path, piece) * piece + row_of_all % piece
    pick = (row_of_held[:, None] == slot_of_row[None, :]).astype(jnp.bfloat16)
    back = (slot_of_row[:, None] == row_of_held[None, :]).astype(jnp.bfloat16)

    def exchange(block):
        w = block.shape[1]
        return lax.all_to_all(
            block.reshape(paths, piece, w), "path", split_axis=0, concat_axis=0, tiled=True
        ).reshape(rows, w)

    outer = outer_params.reshape(held, width)
    moment = momentum.reshape(held, width)
    rows_in = hidden[0]
    z = lax.axis_index("shard")
    tokens = residual.shape[1]
    up = [(i, (i + 1) % shards) for i in range(shards)]
    down = [(i, (i - 1) % shards) for i in range(shards)]
    far = shards // 2
    ring_width = sum(STREAMS)

    received = exchange(trained[0])
    params, moments, sent = update(pick, back, count_of_row, received, outer, moment)
    slab = exchange(sent)

    def add(part, value):
        return (part.astype(jnp.float32) + value.astype(jnp.float32)).astype(jnp.bfloat16)

    class Ring:
        def __init__(self, lo, w, flip):
            self.lo, self.w = lo, w
            self.one, self.other = (down, up) if flip else (up, down)
            self.sign = -1 if flip else 1
            self.ahead, self.behind = self.head(far), self.head(far + 1)

        def head(self, offset):
            at = (z + self.sign * offset) % shards * tokens
            block = lax.dynamic_slice_in_dim(rows_in, at, tokens, 0)
            part = jnp.dot(
                block, slab[:, self.lo:self.lo + self.w], preferred_element_type=jnp.float32
            )
            return part.astype(jnp.bfloat16)

        def run(self, slab, earlier):
            place = ((z + self.sign * jnp.arange(shards, dtype=jnp.int32)) % shards).astype(jnp.int32)
            parts, whole = products(place, rows_in, slab, earlier, self.lo, self.w, shards)
            parts = parts[:far] + [None, None] + parts[far:]
            ahead, behind = self.ahead, self.behind
            for k in range(far - 1, -1, -1):
                ahead = lax.ppermute(ahead, "shard", self.one)
                if k:
                    behind = lax.ppermute(behind, "shard", self.other)
                if k:
                    ahead = add(parts[k], ahead)
                if k > 1:
                    behind = add(parts[shards + 1 - k], behind)
            own = parts[0].astype(jnp.float32)
            own = own + residual[0, :, self.lo:self.lo + self.w].astype(jnp.float32)
            self.total = (own + ahead.astype(jnp.float32) + behind.astype(jnp.float32)).astype(
                jnp.bfloat16
            )
            return [whole]

    rings, lo = [], 0
    for n, w in enumerate(STREAMS):
        rings.append(Ring(lo, w, n % 2 == 1))
        lo += w
    later = after(slab, *[r.ahead for r in rings], *[r.behind for r in rings])
    whole = []
    for r in rings:
        whole = r.run(later, whole)
    mixed = [r.total for r in rings]
    return (
        params.reshape(outer_params.shape),
        moments.reshape(outer_params.shape),
        whole[0][None],
        jnp.concatenate(mixed, axis=1)[None],
    )


def solution(mesh):
    placed = (
        P("path", "shard", None),
        P(None, "shard", "path", None),
        P(None, "shard", "path", None),
        P(),
        P(),
        P("path", None, "shard"),
        P("path", "shard", None),
    )
    return jax.shard_map(
        body,
        mesh=mesh,
        in_specs=placed,
        out_specs=(
            P(None, "shard", "path", None),
            P(None, "shard", "path", None),
            P("path", "shard", None),
            P("path", "shard", None),
        ),
        check_vma=False,
    )
```

```python
import jax
import jax.numpy as jnp
from jax import lax
from jax.experimental import pallas as pl
from jax.experimental.pallas import tpu as pltpu
from jax.sharding import PartitionSpec as P

STREAMS = (768, 768, 512)
WIDE = 256
LIMIT = 12
UPW = 512


def after(value, *others):
    return lax.optimization_barrier((value, *others))[0]


def update_kernel(pick, back, count, received, outer, moment, params, moments, sent):
    totals = jnp.dot(pick[...], received[...], preferred_element_type=jnp.float32)
    pseudo = outer[...] - totals / count[...]
    momentum = 0.9 * moment[...] + pseudo
    new = outer[...] - 0.7 * (pseudo + 0.9 * momentum)
    params[...] = new
    moments[...] = momentum
    sent[...] = jnp.dot(
        back[...], new.astype(jnp.bfloat16), preferred_element_type=jnp.float32
    ).astype(jnp.bfloat16)


def update(pick, back, count, received, outer, moment):
    held, width = outer.shape
    rows = received.shape[0]
    wide = UPW
    fixed = lambda i: (0, 0)
    here = lambda i: (0, i)
    return pl.pallas_call(
        update_kernel,
        grid=(width // wide,),
        in_specs=[
            pl.BlockSpec(pick.shape, fixed),
            pl.BlockSpec(back.shape, fixed),
            pl.BlockSpec(count.shape, fixed),
            pl.BlockSpec((rows, wide), here),
            pl.BlockSpec((held, wide), here),
            pl.BlockSpec((held, wide), here),
        ],
        out_specs=[
            pl.BlockSpec((held, wide), here),
            pl.BlockSpec((held, wide), here),
            pl.BlockSpec((rows, wide), here),
        ],
        out_shape=[
            pltpu.HBM((held, width), jnp.float32),
            pltpu.HBM((held, width), jnp.float32),
            pltpu.HBM((rows, width), jnp.bfloat16),
        ],
        compiler_params=pltpu.CompilerParams(vmem_limit_bytes=LIMIT * 1024 * 1024),
        cost_estimate=pl.CostEstimate(
            flops=4 * held * rows * width,
            bytes_accessed=(rows * 4 + held * 16) * width,
            transcendentals=0,
        ),
        name="update",
    )(pick, back, count, received, outer, moment)


def product_kernel(place, hidden, slab, *rest):
    outs, slabs, total = rest[-8:-2], rest[-2], rest[-1]
    total[...] = jnp.dot(hidden[...], slab[...], preferred_element_type=jnp.float32).astype(
        total.dtype
    )
    slabs[...] = slab[...]
    tokens = outs[0].shape[0]
    shards = hidden.shape[0] // tokens
    far = shards // 2
    for d, out in zip([d for d in range(shards) if d not in (far, far + 1)], outs):
        start = pl.multiple_of(place[d] * tokens, tokens)
        out[...] = total[pl.ds(start, tokens), :]


def products(place, hidden, slab, earlier, at, w, shards):
    rows, width = slab.shape
    tokens = hidden.shape[0] // shards
    wide = WIDE
    first = at // wide
    outs = pl.pallas_call(
        product_kernel,
        grid_spec=pltpu.PrefetchScalarGridSpec(
            num_scalar_prefetch=1,
            grid=(w // wide,),
            in_specs=[
                pl.BlockSpec(hidden.shape, lambda j, p: (0, 0)),
                pl.BlockSpec((rows, wide), lambda j, p: (0, first + j)),
            ]
            + [pl.BlockSpec(memory_space=pl.ANY)] * len(earlier),
            out_specs=[pl.BlockSpec((tokens, wide), lambda j, p: (0, j))] * (shards - 2)
            + [pl.BlockSpec((rows, wide), lambda j, p: (0, first + j))],
            scratch_shapes=[pltpu.VMEM((hidden.shape[0], wide), jnp.bfloat16)],
        ),
        out_shape=[jax.ShapeDtypeStruct((tokens, w), jnp.bfloat16)] * (shards - 2)
        + [pltpu.HBM((rows, width), jnp.bfloat16)],
        input_output_aliases={3: shards - 2} if earlier else {},
        compiler_params=pltpu.CompilerParams(vmem_limit_bytes=LIMIT * 1024 * 1024),
        cost_estimate=pl.CostEstimate(
            flops=2 * hidden.size * w,
            bytes_accessed=2 * (hidden.size + 2 * rows * w + shards * tokens * w),
            transcendentals=0,
        ),
        name="products",
    )(place, hidden, slab, *earlier)
    return list(outs[:-1]), outs[-1]


def finish_kernel(resid, *refs):
    ends, out = refs[:-1], refs[-1]
    at = 0
    for own, ahead, behind in zip(ends[0::3], ends[1::3], ends[2::3]):
        here = slice(at, at + own.shape[1])
        total = own[...].astype(jnp.float32) + resid[:, here].astype(jnp.float32)
        total = total + ahead[...].astype(jnp.float32) + behind[...].astype(jnp.float32)
        out[:, here] = total.astype(jnp.bfloat16)
        at += own.shape[1]


def finish(resid, ends):
    tokens, width = resid.shape
    half = tokens // 2
    rows = lambda i: (i, 0)
    arrays = [value for end in ends for value in end]
    return pl.pallas_call(
        finish_kernel,
        grid=(2,),
        in_specs=[pl.BlockSpec((half, width), rows)]
        + [pl.BlockSpec((half, value.shape[1]), rows) for value in arrays],
        out_specs=pl.BlockSpec((half, width), rows),
        out_shape=jax.ShapeDtypeStruct((tokens, width), jnp.bfloat16),
        compiler_params=pltpu.CompilerParams(vmem_limit_bytes=LIMIT * 1024 * 1024),
        cost_estimate=pl.CostEstimate(
            flops=3 * resid.size, bytes_accessed=10 * resid.size, transcendentals=0
        ),
        name="finish",
    )(resid, *arrays)


def body(trained, outer_params, momentum, path_module, module_slot, hidden, residual):
    paths = lax.axis_size("path")
    shards = lax.axis_size("shard")
    mods = outer_params.shape[0]
    piece = outer_params.shape[2]
    width = outer_params.shape[3]
    rows = paths * piece
    held = mods * piece
    labels = jnp.arange(mods, dtype=jnp.int32)
    slot_of_path = jnp.sum(
        jnp.where(path_module == labels[None, :], module_slot[None, :], 0), axis=1
    )
    choose = slot_of_path[None, :] == labels[:, None]
    counts = jnp.sum(choose.astype(jnp.float32), axis=1)
    count_of_row = jnp.repeat(counts, piece)[:, None]
    row_of_held = jnp.arange(held, dtype=jnp.int32)
    row_of_all = jnp.arange(rows, dtype=jnp.int32)
    slot_of_row = jnp.repeat(slot_of_path, piece) * piece + row_of_all % piece
    pick = (row_of_held[:, None] == slot_of_row[None, :]).astype(jnp.bfloat16)
    back = (slot_of_row[:, None] == row_of_held[None, :]).astype(jnp.bfloat16)

    def exchange(block):
        w = block.shape[1]
        return lax.all_to_all(
            block.reshape(paths, piece, w), "path", split_axis=0, concat_axis=0, tiled=True
        ).reshape(rows, w)

    outer = outer_params.reshape(held, width)
    moment = momentum.reshape(held, width)
    rows_in = hidden[0]
    z = lax.axis_index("shard")
    tokens = residual.shape[1]
    up = [(i, (i + 1) % shards) for i in range(shards)]
    down = [(i, (i - 1) % shards) for i in range(shards)]
    far = shards // 2
    ring_width = sum(STREAMS)

    received = exchange(trained[0])
    params, moments, sent = update(pick, back, count_of_row, received, outer, moment)
    slab = exchange(sent)

    def add(part, value):
        return (part.astype(jnp.float32) + value.astype(jnp.float32)).astype(jnp.bfloat16)

    class Ring:
        def __init__(self, lo, w, flip):
            self.lo, self.w = lo, w
            self.one, self.other = (down, up) if flip else (up, down)
            self.sign = -1 if flip else 1
            self.ahead, self.behind = self.head(far), self.head(far + 1)

        def head(self, offset):
            at = (z + self.sign * offset) % shards * tokens
            block = lax.dynamic_slice_in_dim(rows_in, at, tokens, 0)
            part = jnp.dot(
                block, slab[:, self.lo:self.lo + self.w], preferred_element_type=jnp.float32
            )
            return part.astype(jnp.bfloat16)

        def run(self, slab, earlier):
            place = ((z + self.sign * jnp.arange(shards, dtype=jnp.int32)) % shards).astype(jnp.int32)
            parts, whole = products(place, rows_in, slab, earlier, self.lo, self.w, shards)
            parts = parts[:far] + [None, None] + parts[far:]
            ahead, behind = self.ahead, self.behind
            for k in range(far - 1, -1, -1):
                ahead = lax.ppermute(ahead, "shard", self.one)
                if k:
                    behind = lax.ppermute(behind, "shard", self.other)
                if k:
                    ahead = add(parts[k], ahead)
                if k > 1:
                    behind = add(parts[shards + 1 - k], behind)
            self.ends = (parts[0], ahead, behind)
            return [whole]

    rings, lo = [], 0
    for n, w in enumerate(STREAMS):
        rings.append(Ring(lo, w, n % 2 == 1))
        lo += w
    later = after(slab, *[r.ahead for r in rings], *[r.behind for r in rings])
    whole = []
    for r in rings:
        whole = r.run(later, whole)
    mixed = finish(residual[0], [r.ends for r in rings])
    return (
        params.reshape(outer_params.shape),
        moments.reshape(outer_params.shape),
        whole[0][None],
        mixed[None],
    )


def solution(mesh):
    placed = (
        P("path", "shard", None),
        P(None, "shard", "path", None),
        P(None, "shard", "path", None),
        P(),
        P(),
        P("path", None, "shard"),
        P("path", "shard", None),
    )
    return jax.shard_map(
        body,
        mesh=mesh,
        in_specs=placed,
        out_specs=(
            P(None, "shard", "path", None),
            P(None, "shard", "path", None),
            P("path", "shard", None),
            P("path", "shard", None),
        ),
        check_vma=False,
    )
```
